32 devices in a mesh: row: 8 (over y, x, core), col: 4 (over z).
Axes of the slice: x: 2, y: 2, z: 4, core: 2. Of those that a mesh axis runs over, the one named last changes fastest.
Arguments:
- stored_blocks: float32 [256, 8, 128, 128], P('row', 'col'), may hold values from -1.8 to 1.8
- block_cols: int32 [256, 8], P('row', 'col'), may hold values from 0 to 31, as said below
- storage_map: int32 [256, 8], P('row', 'col'), may hold values from 0 to 1, as said below
Outputs:
- square_part: float32 [256, 8, 128, 128], P('row', 'col')
The draws below stay inside these ranges and needn't reach their ends.
Inputs may be any that keep to these rules, and one draw needn't show every extreme that they name: The block pattern is symmetric: block (R, q) with column C = q * 32 + block_cols[R, q] has block_cols[C, R // 32] == R mod 32; every slab pairs its block rows with its block columns one to one; block_cols[R, R // 32] == R mod 32. Of a block and its mirror image exactly one has storage_map 1; blocks on the diagonal have 1.
All inputs are finite; a program needn't handle non-finite values.
Results may differ from the reference program's by a relative error of at most 0.0001.
Values sent between devices are 32-bit elements; how exact they have to be, the bound alone decides.
A program may use at most 128 MiB of HBM per device.

```python
import jax
import jax.numpy as jnp
from jax import lax

BS = 128
BLK = 32
STEPS = 4
SLABS = 8
NBLK = 256


def build_pattern(key):
    base_key = jax.random.fold_in(key, 7)
    perm_key, shift_key, swap_key, coin_key = jax.random.split(base_key, 4)
    sigma = jax.vmap(lambda k: jax.random.permutation(k, BLK))(jax.random.split(perm_key, SLABS)).astype(jnp.int32)
    inverse = jnp.argsort(sigma, axis=1).astype(jnp.int32)
    offsets = jax.random.randint(shift_key, (SLABS,), 0, BLK).astype(jnp.int32)
    offset_gap = offsets[:, None] - offsets[None, :]
    moved_count = 2 * max(1, BLK // 8)
    slot_ids = jnp.arange(BLK, dtype=jnp.int32)
    partner = jnp.where(slot_ids < moved_count, jnp.bitwise_xor(slot_ids, 1), slot_ids).astype(jnp.int32)

    def make_swap(pair_index):
        shuffled = jax.random.permutation(jax.random.fold_in(swap_key, pair_index), BLK).astype(jnp.int32)
        return jnp.zeros((BLK,), jnp.int32).at[shuffled].set(shuffled[partner])
    slab_ids = jnp.arange(SLABS, dtype=jnp.int32)
    lower_slab = jnp.minimum(slab_ids[:, None], slab_ids[None, :])
    upper_slab = jnp.maximum(slab_ids[:, None], slab_ids[None, :])
    swaps = jax.vmap(make_swap)((lower_slab * SLABS + upper_slab).reshape(-1)).reshape(SLABS, SLABS, BLK)
    diagonal_pair = slab_ids[:, None] == slab_ids[None, :]
    swaps = jnp.where(diagonal_pair[:, :, None], slot_ids[None, None, :], swaps).astype(jnp.int32)
    total_rows = BLK * SLABS
    row_ids = jnp.arange(total_rows, dtype=jnp.int32)
    slab_of = row_ids // BLK
    local_row = row_ids % BLK
    placed = sigma[slab_of, local_row]
    row_gap = offset_gap[slab_of, :]
    pair_swaps = swaps[slab_of]
    start_slot = jnp.broadcast_to(placed[:, None, None], (total_rows, SLABS, 1))
    forward = jnp.take_along_axis(pair_swaps, start_slot, axis=2)[:, :, 0] - row_gap
    back_slot = ((placed[:, None] - row_gap) % BLK)[:, :, None]
    backward = jnp.take_along_axis(pair_swaps, back_slot, axis=2)[:, :, 0]
    upward = slab_of[:, None] < slab_ids[None, :]
    target = jnp.where(upward, forward, backward) % BLK
    cols = inverse[slab_ids[None, :], target].astype(jnp.int32)
    column_global = slab_ids[None, :] * BLK + cols
    row_global = jnp.broadcast_to(row_ids[:, None], cols.shape)
    first_index = jnp.minimum(row_global, column_global)
    second_index = jnp.maximum(row_global, column_global)
    pair_key = (first_index * total_rows + second_index).reshape(-1)
    coins = jax.vmap(lambda p: jax.random.randint(jax.random.fold_in(coin_key, p), (), 0, 2))(pair_key)
    coins = coins.reshape(cols.shape).astype(jnp.int32)
    stored = jnp.where(row_global < column_global, coins, jnp.where(row_global > column_global, 1 - coins, 1))
    return (cols, stored.astype(jnp.int32))


def draw_block_cols(key, part):
    cols, stored = build_pattern(key)
    return cols


def draw_storage_map(key, part):
    cols, stored = build_pattern(key)
    return stored


def block_scale(stream_key, extent, shards, smallest, high):
    level, own = 1.0, jax.random.fold_in(stream_key, 6)
    for position, blocks in shards:
        steps = jnp.exp(jax.random.uniform(jax.random.fold_in(own, position), (blocks,), jnp.float32, smallest / len(shards), high / len(shards)))
        level = level * jnp.repeat(steps, extent[position] // blocks).reshape([-1 if axis == position else 1 for axis in range(len(extent))])
    return level


def noise(own_key, dims, deviation, limit, cuts=(), held_as=jnp.bfloat16):
    factor_of = block_scale(own_key, dims, cuts, -0.22, 0.18) if cuts else 1.0
    result = jax.random.normal(own_key, dims, jnp.float32) * deviation * factor_of
    return jnp.minimum(jnp.maximum(result, -limit), limit).astype(held_as)


def setup_inputs(seed: int = 0) -> dict:
    seeds = jax.random.split(jax.random.key(seed), 4)
    return {
        "stored_blocks": noise(seeds[0], (NBLK, SLABS, BS, BS), 0.3, 1.8, ((0, 8), (1, 4)), jnp.float32),
        "block_cols": draw_block_cols(jax.random.fold_in(seeds[3], 71), 0),
        "storage_map": draw_storage_map(jax.random.fold_in(seeds[3], 71), 0),
    }


def reference(stored_blocks, block_cols, storage_map):
    held = stored_blocks * storage_map.astype(jnp.float32)[:, :, None, None]
    total_rows = held.shape[0]
    row_ids = jnp.arange(total_rows, dtype=jnp.int32)
    slab_ids = jnp.arange(SLABS, dtype=jnp.int32)
    mirror_rows = slab_ids[None, :] * BLK + block_cols
    mirror_slabs = jnp.broadcast_to((row_ids // BLK)[:, None], block_cols.shape)
    mirrored = held[mirror_rows, mirror_slabs]
    density = held + jnp.swapaxes(mirrored, 2, 3)
    total = jnp.zeros(held.shape, jnp.float32)
    for step in range(STEPS):
        kappa = ((row_ids // BLK + step) % SLABS).astype(jnp.int32)
        left = density[row_ids, kappa]
        inner = (kappa * BLK + block_cols[row_ids, kappa]).astype(jnp.int32)
        right = density[inner]
        match = block_cols[inner] == block_cols
        term = jnp.einsum('rik,rqkj->rqij', left, right, precision=lax.Precision.HIGHEST)
        total = total + jnp.where(match[:, :, None, None], term, jnp.float32(0.0))
    return total
```

```python
import functools

import jax
import jax.numpy as jnp
from jax import lax
from jax.experimental import pallas as pl
from jax.experimental.pallas import tpu as pltpu
from jax.sharding import PartitionSpec as P

STEPS = 4
CHUNKS = 4
MESH = pl.DeviceIdType.MESH


def kernel(n_row, n_col, x_ref, cols_ref, map_ref, out_ref, arr, relay, dens, panels, lefts,
           dir_s, dir_r, rel_s, rel_r, fwd_s, last_s, last_r, self_s,
           pan_s, pan_r, own_s, left_s, left_r):
    blk, groups = x_ref.shape[0], x_ref.shape[1]
    bs = x_ref.shape[2]
    slabs = n_row
    half = blk // 2
    part = blk // CHUNKS
    r, c = lax.axis_index("row"), lax.axis_index("col")
    home, slot = r // groups, r % groups
    core = r % 2

    def remote(src, dst, ss, rs, row, col):
        return pltpu.make_async_remote_copy(
            src_ref=src, dst_ref=dst, send_sem=ss, recv_sem=rs, device_id=(row, col), device_id_type=MESH)

    barrier = pltpu.get_barrier_semaphore()

    @pl.loop(1, n_col)
    def _(d):
        pl.semaphore_signal(barrier, inc=1, device_id=(r, (c + d) % n_col), device_id_type=MESH)

    @pl.loop(1, n_row)
    def _(d):
        pl.semaphore_signal(barrier, inc=1, device_id=((r + d) % n_row, c), device_id_type=MESH)

    @pl.when(home != c)
    def _():
        for g in range(groups):
            pl.semaphore_signal(barrier, inc=1, device_id=(c * groups + g, home), device_id_type=MESH)
        pl.semaphore_wait(barrier, n_col + n_row - 2 + groups)

    @pl.when(home == c)
    def _():
        pl.semaphore_wait(barrier, n_col + n_row - 2)

    lo, hi = pl.ds(0, half), pl.ds(half, half)

    def land(copy, *place):
        for sl in range(groups):
            @pl.when(slot == sl)
            def _(sl=sl):
                copy(*place, arr[sl]).start()

    def direct(g, tile=arr[0]):
        return remote(x_ref.at[lo, g], tile.at[lo], dir_s.at[g], dir_r.at[slot], c * groups + g, home)

    def to_relay(g):
        return remote(x_ref.at[hi, g], relay.at[c, g], rel_s.at[g], rel_r.at[c, g], r, home)

    def last(g, tile=arr[0]):
        return remote(x_ref.at[hi, g], tile.at[hi], rel_s.at[g], last_r.at[slot], c * groups + g, home)

    def forward(c2, g, tile=arr[0]):
        return remote(relay.at[c2, g], tile.at[hi], fwd_s.at[c2, g], last_r.at[slot], c2 * groups + g, c)

    def own(g):
        return pltpu.make_async_copy(x_ref.at[:, g], arr[g], self_s)

    for g in range(groups):
        @pl.when(home != c)
        def _(g=g):
            to_relay(g).start()

        @pl.when((home == c) & (c * groups + g != r))
        def _(g=g):
            land(last, g)

        @pl.when(c * groups + g != r)
        def _(g=g):
            land(direct, g)

        @pl.when(c * groups + g == r)
        def _(g=g):
            own(g).start()

    @pl.when(home == c)
    def _():
        @pl.loop(1, n_col)
        def _(d):
            c2 = (c + d) % n_col
            for g in range(groups):
                pltpu.make_async_copy(relay.at[c2, g], relay.at[c2, g], rel_r.at[c2, g]).wait()
                land(forward, c2, g)

    def recv(ref, sem):
        pltpu.make_async_copy(ref, ref, sem).wait()

    def panel_two(g):
        return remote(dens.at[:, g], panels.at[1, :, g], pan_s.at[0, g], pan_r.at[1, g], (r + n_row - 2) % n_row, c)

    def panel_sib(g):
        return remote(dens.at[:, g], panels.at[0, :, g], pan_s.at[1, g], pan_r.at[0, g], (r + n_row - 1) % n_row, c)

    def panel_far(g):
        return remote(dens.at[:, g], panels.at[2, :, g], pan_s.at[1, g], pan_r.at[2, g], (r + n_row - 3) % n_row, c)

    def pass_on(g, s):
        return remote(panels.at[1, :, g], panels.at[s, :, g], pan_s.at[2, g], pan_r.at[s, g], r + 1 - 2 * core, c)

    def kappa(s):
        return (r + s) % n_row

    def left_from(s, ch, src, side):
        return remote(src, lefts.at[s, pl.ds(ch * part, part)], left_s.at[s, ch, side], left_r.at[s, ch],
                      r, c + 1 - 2 * side)

    def own_left(s):
        return pltpu.make_async_copy(dens.at[:, kappa(s) % groups], lefts.at[s], own_s.at[s])

    row0 = r * blk
    for g in range(groups):
        q = c * groups + g

        @pl.when(q == r)
        def _(g=g):
            own(g).wait()

        @pl.when(q != r)
        def _(g=g):
            recv(arr[g].at[lo], dir_r.at[g])
            recv(arr[g].at[hi], last_r.at[g])

        on_diag = jnp.where(q == r, 1, 0)

        @pl.loop(0, blk)
        def _(i, g=g, q=q, on_diag=on_diag):
            there = cols_ref[(row0 + i) * slabs + q]
            here = map_ref[i * groups + g]
            same = on_diag * jnp.where(there == i, 1, 0)
            mine = here.astype(jnp.float32)
            other = (1 - here + here * same).astype(jnp.float32)
            dens[i, g] = x_ref[i, g] * mine + arr[g][there].T * other

        for s in range(STEPS):
            @pl.when(kappa(s) == q)
            def _(s=s, g=g):
                for ch in range(CHUNKS):
                    src = dens.at[pl.ds(ch * part, part), g]

                    @pl.when(c + 1 < n_col)
                    def _(src=src, ch=ch, s=s):
                        left_from(s, ch, src, 0).start()

                    @pl.when(c > 0)
                    def _(src=src, ch=ch, s=s):
                        left_from(s, ch, src, 1).start()
                own_left(s).start()

        panel_two(g).start()

        @pl.when(core == 1)
        def _(g=g):
            panel_sib(g).start()

        @pl.when(core == 0)
        def _(g=g):
            panel_far(g).start()

    @pl.loop(1, n_col)
    def _(d):
        for s in range(STEPS):
            h = kappa(s) // groups

            @pl.when(h + d == c)
            def _(s=s):
                for ch in range(CHUNKS):
                    piece = lefts.at[s, pl.ds(ch * part, part)]
                    recv(piece, left_r.at[s, ch])

                    @pl.when(c + 1 < n_col)
                    def _(s=s, ch=ch, piece=piece):
                        left_from(s, ch, piece, 0).start()

            @pl.when(c + d == h)
            def _(s=s):
                for ch in range(CHUNKS):
                    piece = lefts.at[s, pl.ds(ch * part, part)]
                    recv(piece, left_r.at[s, ch])

                    @pl.when(c > 0)
                    def _(s=s, ch=ch, piece=piece):
                        left_from(s, ch, piece, 1).start()

    for g in range(groups):
        recv(panels.at[1, :, g], pan_r.at[1, g])

        @pl.when(core == 0)
        def _(g=g):
            pass_on(g, 0).start()

        @pl.when(core == 1)
        def _(g=g):
            pass_on(g, 2).start()

    for s in range(STEPS):
        @pl.when(kappa(s) // groups == c)
        def _(s=s):
            own_left(s).wait()

    for g in range(groups):
        recv(panels.at[0, :, g], pan_r.at[0, g])
        recv(panels.at[2, :, g], pan_r.at[2, g])

    @pl.loop(0, blk)
    def _(i):
        wide, tall = [], []
        for s in range(STEPS):
            k = kappa(s)
            inner = cols_ref[(row0 + i) * slabs + k]
            a = lefts[s, i]
            a_hi = a.astype(jnp.bfloat16)
            a_lo = (a - a_hi.astype(jnp.float32)).astype(jnp.bfloat16)
            tops, lows = [], []
            for g in range(groups):
                q = c * groups + g
                fits = cols_ref[(k * blk + inner) * slabs + q] == cols_ref[(row0 + i) * slabs + q]
                b = dens[inner, g] if s == 0 else panels[s - 1, inner, g]
                b = b * jnp.where(fits, 1, 0).astype(jnp.float32)
                b_hi = b.astype(jnp.bfloat16)
                tops.append(b_hi)
                lows.append((b - b_hi.astype(jnp.float32)).astype(jnp.bfloat16))
            top, low = jnp.concatenate(tops, axis=1), jnp.concatenate(lows, axis=1)
            wide += [a_hi, a_lo, a_hi]
            tall += [top, top, low]
        total = jnp.dot(jnp.concatenate(wide, axis=1), jnp.concatenate(tall, axis=0),
                        preferred_element_type=jnp.float32)
        for g in range(groups):
            out_ref[i, g] = total[:, g * bs:(g + 1) * bs]

    for g in range(groups):
        @pl.when(home != c)
        def _(g=g):
            to_relay(g).wait_send()

        @pl.when((home == c) & (c * groups + g != r))
        def _(g=g):
            last(g).wait_send()

        @pl.when(c * groups + g != r)
        def _(g=g):
            direct(g).wait_send()

        panel_two(g).wait_send()
        panel_sib(g).wait_send()
        pass_on(g, 0).wait_send()

    @pl.when(home == c)
    def _():
        @pl.loop(1, n_col)
        def _(d):
            for g in range(groups):
                forward((c + d) % n_col, g).wait_send()

    for s in range(STEPS):
        h = kappa(s) // groups
        for ch in range(CHUNKS):
            piece = lefts.at[s, pl.ds(ch * part, part)]

            @pl.when((c >= h) & (c + 1 < n_col))
            def _(s=s, ch=ch, piece=piece):
                left_from(s, ch, piece, 0).wait_send()

            @pl.when((c <= h) & (c > 0))
            def _(s=s, ch=ch, piece=piece):
                left_from(s, ch, piece, 1).wait_send()


def shards(n_row, n_col, x, block_cols, storage_map):
    blk, groups, bs = x.shape[0], x.shape[1], x.shape[2]
    cols = lax.all_gather(block_cols, "col", axis=1, tiled=True)
    cols = lax.all_gather(cols, "row", axis=0, tiled=True).reshape(-1)
    f32, dma = jnp.float32, pltpu.SemaphoreType.DMA
    vmem, smem = pl.BlockSpec(memory_space=pltpu.VMEM), pl.BlockSpec(memory_space=pltpu.SMEM)
    return pl.pallas_call(
        functools.partial(kernel, n_row, n_col),
        out_shape=jax.ShapeDtypeStruct(x.shape, f32),
        in_specs=[vmem, smem, smem],
        out_specs=vmem,
        scratch_shapes=[
            [pltpu.VMEM((blk, bs, bs), f32)] * groups,
            pltpu.VMEM((n_col, groups, blk // 2, bs, bs), f32),
            pltpu.VMEM((blk, groups, bs, bs), f32),
            pltpu.VMEM((STEPS - 1, blk, groups, bs, bs), f32),
            pltpu.VMEM((STEPS, blk, bs, bs), f32),
            dma((groups,)), dma((groups,)), dma((groups,)), dma((n_col, groups)), dma((n_col, groups)),
            dma((groups,)), dma((groups,)), dma,
            dma((3, groups)), dma((STEPS - 1, groups)), dma((STEPS,)),
            dma((STEPS, CHUNKS, 2)), dma((STEPS, CHUNKS)),
        ],
        compiler_params=pltpu.CompilerParams(
            collective_id=0, has_side_effects=True, vmem_limit_bytes=56 * 2**20),
    )(x, cols, storage_map.reshape(-1))


def solution(mesh):
    return jax.shard_map(
        functools.partial(shards, mesh.shape["row"], mesh.shape["col"]),
        mesh=mesh,
        in_specs=(P("row", "col", None, None), P("row", "col"), P("row", "col")),
        out_specs=P("row", "col", None, None),
        check_vma=False,
    )
```

```python
import functools

import jax
import jax.numpy as jnp
from jax import lax
from jax.experimental import pallas as pl
from jax.experimental.pallas import tpu as pltpu
from jax.sharding import PartitionSpec as P

STEPS = 4
CHUNKS = 4
MESH = pl.DeviceIdType.MESH


def kernel(n_row, n_col, x_ref, cols_ref, map_ref, out_ref, arr, relay, dens, panels, lefts,
           out_s, in_r, rel_r, fwd_s, self_s,
           pan_s, pan_r, own_s, left_s, left_r):
    blk, groups = x_ref.shape[0], x_ref.shape[1]
    bs = x_ref.shape[2]
    half = blk // 2
    part = blk // CHUNKS
    bit = half // CHUNKS
    r, c = lax.axis_index("row"), lax.axis_index("col")
    home, slot = r // groups, r % groups
    core = r % 2

    def remote(src, dst, ss, rs, row, col):
        return pltpu.make_async_remote_copy(
            src_ref=src, dst_ref=dst, send_sem=ss, recv_sem=rs, device_id=(row, col), device_id_type=MESH)

    barrier = pltpu.get_barrier_semaphore()

    me, devices = r * n_col + c, n_row * n_col

    @pl.loop(1, devices)
    def _(d):
        peer = (me + d) % devices
        pl.semaphore_signal(barrier, inc=1, device_id=(peer // n_col, peer % n_col), device_id_type=MESH)

    pl.semaphore_wait(barrier, devices - 1)

    def recv(ref, sem):
        pltpu.make_async_copy(ref, ref, sem).wait()

    lo, hi = pl.ds(0, half), pl.ds(half, half)

    def land(copy, *place):
        for sl in range(groups):
            @pl.when(slot == sl)
            def _(sl=sl):
                copy(*place, arr[sl]).start()

    chip = r // 2

    def target(c2, g):
        return c2 * groups + g

    def bend(g, way):
        aim = target(c, g) // 2
        if way == 0:
            return chip % 2 != aim % 2, (chip // 2 * 2 + aim % 2) * 2 + core
        return chip // 2 != aim // 2, (aim // 2 * 2 + chip % 2) * 2 + core

    part_of = (lo, hi)

    def direct(g, way, tile=arr[0]):
        return remote(x_ref.at[part_of[way], g], tile.at[part_of[way]], out_s.at[way, g], in_r.at[way, slot],
                      target(c, g), home)

    def to_relay(g, way, ch):
        return remote(x_ref.at[pl.ds(way * half + ch * bit, bit), g], relay.at[chip, g, pl.ds(ch * bit, bit)],
                      out_s.at[way, g], rel_r.at[chip, g, ch], bend(g, way)[1], c)

    def passes(p, g, way):
        aim = target(c, g) // 2
        if way == 0:
            return (p // 2 == chip // 2) & (p % 2 != chip % 2) & (aim % 2 == chip % 2)
        return (p % 2 == chip % 2) & (p // 2 != chip // 2) & (aim // 2 == chip // 2)

    def forward(p, g, way, ch, sl):
        return remote(relay.at[p, g, pl.ds(ch * bit, bit)], arr[sl].at[pl.ds(way * half + ch * bit, bit)],
                      fwd_s.at[p, g], in_r.at[way, sl], target(c, g), (2 * p + core) // groups)

    def own(g):
        return pltpu.make_async_copy(x_ref.at[:, g], arr[g], self_s)

    for g in range(groups):
        for way in range(2):
            turns = bend(g, way)[0]

            @pl.when(turns & (target(c, g) != r))
            def _(g=g, way=way):
                for ch in range(CHUNKS):
                    to_relay(g, way, ch).start()

            @pl.when(jnp.logical_not(turns) & (target(c, g) != r))
            def _(g=g, way=way):
                land(direct, g, way)

        @pl.when(target(c, g) == r)
        def _(g=g):
            own(g).start()

    for ch in range(CHUNKS):
        @pl.loop(0, n_row // 2)
        def _(p, ch=ch):
            for g in range(groups):
                for way in range(2):
                    @pl.when(passes(p, g, way))
                    def _(g=g, way=way):
                        recv(relay.at[p, g, pl.ds(ch * bit, bit)], rel_r.at[p, g, ch])
                        for sl in range(groups):
                            @pl.when((2 * p + core) % groups == sl)
                            def _(sl=sl):
                                forward(p, g, way, ch, sl).start()

    def panel_two(g):
        return remote(dens.at[:, g], panels.at[1, :, g], pan_s.at[0, g], pan_r.at[1, g], (r + n_row - 2) % n_row, c)

    def panel_sib(g):
        return remote(dens.at[:, g], panels.at[0, :, g], pan_s.at[1, g], pan_r.at[0, g], (r + n_row - 1) % n_row, c)

    def panel_far(g):
        return remote(dens.at[:, g], panels.at[2, :, g], pan_s.at[1, g], pan_r.at[2, g], (r + n_row - 3) % n_row, c)

    def pass_on(g, s):
        return remote(panels.at[1, :, g], panels.at[s, :, g], pan_s.at[2, g], pan_r.at[s, g], r + 1 - 2 * core, c)

    def col_of(k, i, q):
        return cols_ref[((k * n_col + q // groups) * blk + i) * groups + q % groups]

    def kappa(s):
        return (r + s) % n_row

    def left_from(s, ch, src, side):
        return remote(src, lefts.at[s, pl.ds(ch * part, part)], left_s.at[s, ch, side], left_r.at[s, ch],
                      r, c + 1 - 2 * side)

    def own_left(s):
        return pltpu.make_async_copy(dens.at[:, kappa(s) % groups], lefts.at[s], own_s.at[s])

    for g in range(groups):
        q = c * groups + g

        @pl.when(q == r)
        def _(g=g):
            own(g).wait()

        @pl.when(q != r)
        def _(g=g):
            recv(arr[g].at[lo], in_r.at[0, g])
            recv(arr[g].at[hi], in_r.at[1, g])

        on_diag = jnp.where(q == r, 1, 0)

        @pl.loop(0, blk)
        def _(i, g=g, q=q, on_diag=on_diag):
            there = col_of(r, i, q)
            here = map_ref[i * groups + g]
            same = on_diag * jnp.where(there == i, 1, 0)
            mine = here.astype(jnp.float32)
            other = (1 - here + here * same).astype(jnp.float32)
            dens[i, g] = x_ref[i, g] * mine + arr[g][there].T * other

        for s in range(STEPS):
            @pl.when(kappa(s) == q)
            def _(s=s, g=g):
                for ch in range(CHUNKS):
                    src = dens.at[pl.ds(ch * part, part), g]

                    @pl.when(c + 1 < n_col)
                    def _(src=src, ch=ch, s=s):
                        left_from(s, ch, src, 0).start()

                    @pl.when(c > 0)
                    def _(src=src, ch=ch, s=s):
                        left_from(s, ch, src, 1).start()
                own_left(s).start()

        panel_two(g).start()

        @pl.when(core == 1)
        def _(g=g):
            panel_sib(g).start()

        @pl.when(core == 0)
        def _(g=g):
            panel_far(g).start()

    @pl.loop(1, n_col)
    def _(d):
        for s in range(STEPS):
            h = kappa(s) // groups

            @pl.when(h + d == c)
            def _(s=s):
                for ch in range(CHUNKS):
                    piece = lefts.at[s, pl.ds(ch * part, part)]
                    recv(piece, left_r.at[s, ch])

                    @pl.when(c + 1 < n_col)
                    def _(s=s, ch=ch, piece=piece):
                        left_from(s, ch, piece, 0).start()

            @pl.when(c + d == h)
            def _(s=s):
                for ch in range(CHUNKS):
                    piece = lefts.at[s, pl.ds(ch * part, part)]
                    recv(piece, left_r.at[s, ch])

                    @pl.when(c > 0)
                    def _(s=s, ch=ch, piece=piece):
                        left_from(s, ch, piece, 1).start()

    for g in range(groups):
        recv(panels.at[1, :, g], pan_r.at[1, g])

        @pl.when(core == 0)
        def _(g=g):
            pass_on(g, 0).start()

        @pl.when(core == 1)
        def _(g=g):
            pass_on(g, 2).start()

    for s in range(STEPS):
        @pl.when(kappa(s) // groups == c)
        def _(s=s):
            own_left(s).wait()

    for g in range(groups):
        recv(panels.at[0, :, g], pan_r.at[0, g])
        recv(panels.at[2, :, g], pan_r.at[2, g])

    @pl.loop(0, blk)
    def _(i):
        wide, tall = [], []
        for s in range(STEPS):
            k = kappa(s)
            inner = col_of(r, i, k)
            a = lefts[s, i]
            a_hi = a.astype(jnp.bfloat16)
            a_lo = (a - a_hi.astype(jnp.float32)).astype(jnp.bfloat16)
            tops, lows = [], []
            for g in range(groups):
                q = c * groups + g
                fits = col_of(k, inner, q) == col_of(r, i, q)
                b = dens[inner, g] if s == 0 else panels[s - 1, inner, g]
                b = b * jnp.where(fits, 1, 0).astype(jnp.float32)
                b_hi = b.astype(jnp.bfloat16)
                tops.append(b_hi)
                lows.append((b - b_hi.astype(jnp.float32)).astype(jnp.bfloat16))
            top, low = jnp.concatenate(tops, axis=1), jnp.concatenate(lows, axis=1)
            wide += [a_hi, a_lo, a_hi]
            tall += [top, top, low]
        total = jnp.dot(jnp.concatenate(wide, axis=1), jnp.concatenate(tall, axis=0),
                        preferred_element_type=jnp.float32)
        for g in range(groups):
            out_ref[i, g] = total[:, g * bs:(g + 1) * bs]

    for g in range(groups):
        @pl.when(target(c, g) != r)
        def _(g=g):
            for way in range(2):
                direct(g, way).wait_send()

        panel_two(g).wait_send()
        panel_sib(g).wait_send()
        pass_on(g, 0).wait_send()

    @pl.loop(0, n_row // 2)
    def _(p):
        for g in range(groups):
            @pl.when(passes(p, g, 0) | passes(p, g, 1))
            def _(g=g):
                pltpu.make_async_copy(relay.at[p, g], relay.at[p, g], fwd_s.at[p, g]).wait()

    for s in range(STEPS):
        h = kappa(s) // groups
        for ch in range(CHUNKS):
            piece = lefts.at[s, pl.ds(ch * part, part)]

            @pl.when((c >= h) & (c + 1 < n_col))
            def _(s=s, ch=ch, piece=piece):
                left_from(s, ch, piece, 0).wait_send()

            @pl.when((c <= h) & (c > 0))
            def _(s=s, ch=ch, piece=piece):
                left_from(s, ch, piece, 1).wait_send()


def shards(n_row, n_col, x, block_cols, storage_map):
    blk, groups, bs = x.shape[0], x.shape[1], x.shape[2]
    cols = lax.all_gather(block_cols, ("row", "col"), axis=0, tiled=True).reshape(-1)
    f32, dma = jnp.float32, pltpu.SemaphoreType.DMA
    vmem, smem = pl.BlockSpec(memory_space=pltpu.VMEM), pl.BlockSpec(memory_space=pltpu.SMEM)
    return pl.pallas_call(
        functools.partial(kernel, n_row, n_col),
        out_shape=jax.ShapeDtypeStruct(x.shape, f32),
        in_specs=[vmem, smem, smem],
        out_specs=vmem,
        scratch_shapes=[
            [pltpu.VMEM((blk, bs, bs), f32)] * groups,
            pltpu.VMEM((n_row // 2, groups, blk // 2, bs, bs), f32),
            pltpu.VMEM((blk, groups, bs, bs), f32),
            pltpu.VMEM((STEPS - 1, blk, groups, bs, bs), f32),
            pltpu.VMEM((STEPS, blk, bs, bs), f32),
            dma((2, groups)), dma((2, groups)), dma((n_row // 2, groups, CHUNKS)), dma((n_row // 2, groups)), dma,
            dma((3, groups)), dma((STEPS - 1, groups)), dma((STEPS,)),
            dma((STEPS, CHUNKS, 2)), dma((STEPS, CHUNKS)),
        ],
        compiler_params=pltpu.CompilerParams(
            collective_id=0, has_side_effects=True, vmem_limit_bytes=56 * 2**20),
    )(x, cols, storage_map.reshape(-1))


def solution(mesh):
    return jax.shard_map(
        functools.partial(shards, mesh.shape["row"], mesh.shape["col"]),
        mesh=mesh,
        in_specs=(P("row", "col", None, None), P("row", "col"), P("row", "col")),
        out_specs=P("row", "col", None, None),
        check_vma=False,
    )
```

```python
import functools

import jax
import jax.numpy as jnp
from jax import lax
from jax.experimental import pallas as pl
from jax.experimental.pallas import tpu as pltpu
from jax.sharding import PartitionSpec as P

STEPS = 4
CHUNKS = 4
MESH = pl.DeviceIdType.MESH


def kernel(n_row, n_col, x_ref, cols_ref, map_ref, out_ref, arr, relay, dens, panels, lefts,
           out_s, in_r, rel_r, fwd_s, self_s,
           pan_s, pan_r, own_s, left_s, left_r):
    blk, groups = x_ref.shape[0], x_ref.shape[1]
    bs = x_ref.shape[2]
    half = blk // 2
    part = blk // CHUNKS
    bit = half // CHUNKS
    r, c = lax.axis_index("row"), lax.axis_index("col")
    home, slot = r // groups, r % groups
    core = r % 2

    def remote(src, dst, ss, rs, row, col):
        return pltpu.make_async_remote_copy(
            src_ref=src, dst_ref=dst, send_sem=ss, recv_sem=rs, device_id=(row, col), device_id_type=MESH)

    barrier = pltpu.get_barrier_semaphore()

    me, devices = r * n_col + c, n_row * n_col

    @pl.loop(1, devices)
    def _(d):
        peer = (me + d) % devices
        pl.semaphore_signal(barrier, inc=1, device_id=(peer // n_col, peer % n_col), device_id_type=MESH)

    pl.semaphore_wait(barrier, devices - 1)

    def recv(ref, sem):
        pltpu.make_async_copy(ref, ref, sem).wait()

    lo, hi = pl.ds(0, half), pl.ds(half, half)

    def land(copy, *place):
        for sl in range(groups):
            @pl.when(slot == sl)
            def _(sl=sl):
                copy(*place, arr[sl]).start()

    chip = r // 2

    def target(c2, g):
        return c2 * groups + g

    def bend(g, way):
        aim = target(c, g) // 2
        if way == 0:
            return chip % 2 != aim % 2, (chip // 2 * 2 + aim % 2) * 2 + core
        return chip // 2 != aim // 2, (aim // 2 * 2 + chip % 2) * 2 + core

    part_of = (lo, hi)

    def direct(g, way, tile=arr[0]):
        return remote(x_ref.at[part_of[way], g], tile.at[part_of[way]], out_s.at[way, g], in_r.at[way, slot],
                      target(c, g), home)

    def to_relay(g, way, ch):
        return remote(x_ref.at[pl.ds(way * half + ch * bit, bit), g], relay.at[chip, g, pl.ds(ch * bit, bit)],
                      out_s.at[way, g], rel_r.at[chip, g, ch], bend(g, way)[1], c)

    def passes(p, g, way):
        aim = target(c, g) // 2
        if way == 0:
            return (p // 2 == chip // 2) & (p % 2 != chip % 2) & (aim % 2 == chip % 2)
        return (p % 2 == chip % 2) & (p // 2 != chip // 2) & (aim // 2 == chip // 2)

    def forward(p, g, way, ch, sl):
        return remote(relay.at[p, g, pl.ds(ch * bit, bit)], arr[sl].at[pl.ds(way * half + ch * bit, bit)],
                      fwd_s.at[p, g], in_r.at[way, sl], target(c, g), (2 * p + core) // groups)

    def own(g):
        return pltpu.make_async_copy(x_ref.at[:, g], arr[g], self_s)

    for g in range(groups):
        for way in range(2):
            turns = bend(g, way)[0]

            @pl.when(turns & (target(c, g) != r))
            def _(g=g, way=way):
                for ch in range(CHUNKS):
                    to_relay(g, way, ch).start()

            @pl.when(jnp.logical_not(turns) & (target(c, g) != r))
            def _(g=g, way=way):
                land(direct, g, way)

        @pl.when(target(c, g) == r)
        def _(g=g):
            own(g).start()

    for ch in range(CHUNKS):
        @pl.loop(0, n_row // 2)
        def _(p, ch=ch):
            for g in range(groups):
                for way in range(2):
                    @pl.when(passes(p, g, way))
                    def _(g=g, way=way):
                        recv(relay.at[p, g, pl.ds(ch * bit, bit)], rel_r.at[p, g, ch])
                        for sl in range(groups):
                            @pl.when((2 * p + core) % groups == sl)
                            def _(sl=sl):
                                forward(p, g, way, ch, sl).start()

    def panel_two(g):
        return remote(dens.at[:, g], panels.at[1, :, g], pan_s.at[0, g], pan_r.at[1, g], (r + n_row - 2) % n_row, c)

    def panel_sib(g):
        return remote(dens.at[:, g], panels.at[0, :, g], pan_s.at[1, g], pan_r.at[0, g], (r + n_row - 1) % n_row, c)

    def panel_far(g):
        return remote(dens.at[:, g], panels.at[2, :, g], pan_s.at[1, g], pan_r.at[2, g], (r + n_row - 3) % n_row, c)

    def pass_on(g, s):
        return remote(panels.at[1, :, g], panels.at[s, :, g], pan_s.at[2, g], pan_r.at[s, g], r + 1 - 2 * core, c)

    def col_of(k, i, q):
        return cols_ref[(k * blk + i) * n_col * groups + q]

    def kappa(s):
        return (r + s) % n_row

    def left_from(s, ch, src, side):
        return remote(src, lefts.at[s, pl.ds(ch * part, part)], left_s.at[s, ch, side], left_r.at[s, ch],
                      r, c + 1 - 2 * side)

    def own_left(s):
        return pltpu.make_async_copy(dens.at[:, kappa(s) % groups], lefts.at[s], own_s.at[s])

    for g in range(groups):
        q = c * groups + g

        @pl.when(q == r)
        def _(g=g):
            own(g).wait()

        @pl.when(q != r)
        def _(g=g):
            recv(arr[g].at[lo], in_r.at[0, g])
            recv(arr[g].at[hi], in_r.at[1, g])

        on_diag = jnp.where(q == r, 1, 0)

        @pl.loop(0, blk, unroll=4)
        def _(i, g=g, q=q, on_diag=on_diag):
            there = col_of(r, i, q)
            here = map_ref[i * groups + g]
            same = on_diag * jnp.where(there == i, 1, 0)
            mine = here.astype(jnp.float32)
            other = (1 - here + here * same).astype(jnp.float32)
            dens[i, g] = x_ref[i, g] * mine + arr[g][there].T * other

        for s in range(STEPS):
            @pl.when(kappa(s) == q)
            def _(s=s, g=g):
                for ch in range(CHUNKS):
                    src = dens.at[pl.ds(ch * part, part), g]

                    @pl.when(c + 1 < n_col)
                    def _(src=src, ch=ch, s=s):
                        left_from(s, ch, src, 0).start()

                    @pl.when(c > 0)
                    def _(src=src, ch=ch, s=s):
                        left_from(s, ch, src, 1).start()
                own_left(s).start()

        panel_two(g).start()

        @pl.when(core == 1)
        def _(g=g):
            panel_sib(g).start()

        @pl.when(core == 0)
        def _(g=g):
            panel_far(g).start()

    @pl.loop(1, n_col)
    def _(d):
        for s in range(STEPS):
            h = kappa(s) // groups

            @pl.when(h + d == c)
            def _(s=s):
                for ch in range(CHUNKS):
                    piece = lefts.at[s, pl.ds(ch * part, part)]
                    recv(piece, left_r.at[s, ch])

                    @pl.when(c + 1 < n_col)
                    def _(s=s, ch=ch, piece=piece):
                        left_from(s, ch, piece, 0).start()

            @pl.when(c + d == h)
            def _(s=s):
                for ch in range(CHUNKS):
                    piece = lefts.at[s, pl.ds(ch * part, part)]
                    recv(piece, left_r.at[s, ch])

                    @pl.when(c > 0)
                    def _(s=s, ch=ch, piece=piece):
                        left_from(s, ch, piece, 1).start()

    for g in range(groups):
        recv(panels.at[1, :, g], pan_r.at[1, g])

        @pl.when(core == 0)
        def _(g=g):
            pass_on(g, 0).start()

        @pl.when(core == 1)
        def _(g=g):
            pass_on(g, 2).start()

    for s in range(STEPS):
        @pl.when(kappa(s) // groups == c)
        def _(s=s):
            own_left(s).wait()

    for g in range(groups):
        recv(panels.at[0, :, g], pan_r.at[0, g])
        recv(panels.at[2, :, g], pan_r.at[2, g])

    @pl.loop(0, blk, unroll=2)
    def _(i):
        wide, tall = [], []
        for s in range(STEPS):
            k = kappa(s)
            inner = col_of(r, i, k)
            a = lefts[s, i]
            a_hi = a.astype(jnp.bfloat16)
            a_lo = (a - a_hi.astype(jnp.float32)).astype(jnp.bfloat16)
            tops, lows = [], []
            for g in range(groups):
                q = c * groups + g
                fits = col_of(k, inner, q) == col_of(r, i, q)
                b = dens[inner, g] if s == 0 else panels[s - 1, inner, g]
                b = b * jnp.where(fits, 1, 0).astype(jnp.float32)
                b_hi = b.astype(jnp.bfloat16)
                tops.append(b_hi)
                lows.append((b - b_hi.astype(jnp.float32)).astype(jnp.bfloat16))
            top, low = jnp.concatenate(tops, axis=1), jnp.concatenate(lows, axis=1)
            wide += [a_hi, a_lo, a_hi]
            tall += [top, top, low]
        total = jnp.dot(jnp.concatenate(wide, axis=1), jnp.concatenate(tall, axis=0),
                        preferred_element_type=jnp.float32)
        for g in range(groups):
            out_ref[i, g] = total[:, g * bs:(g + 1) * bs]

    for g in range(groups):
        @pl.when(target(c, g) != r)
        def _(g=g):
            for way in range(2):
                direct(g, way).wait_send()

        panel_two(g).wait_send()
        panel_sib(g).wait_send()
        pass_on(g, 0).wait_send()

    @pl.loop(0, n_row // 2)
    def _(p):
        for g in range(groups):
            @pl.when(passes(p, g, 0) | passes(p, g, 1))
            def _(g=g):
                pltpu.make_async_copy(relay.at[p, g], relay.at[p, g], fwd_s.at[p, g]).wait()

    for s in range(STEPS):
        h = kappa(s) // groups
        for ch in range(CHUNKS):
            piece = lefts.at[s, pl.ds(ch * part, part)]

            @pl.when((c >= h) & (c + 1 < n_col))
            def _(s=s, ch=ch, piece=piece):
                left_from(s, ch, piece, 0).wait_send()

            @pl.when((c <= h) & (c > 0))
            def _(s=s, ch=ch, piece=piece):
                left_from(s, ch, piece, 1).wait_send()


def shards(n_row, n_col, x, block_cols, storage_map):
    blk, groups, bs = x.shape[0], x.shape[1], x.shape[2]
    cols = lax.all_gather(block_cols, "col", axis=1, tiled=True)
    cols = lax.all_gather(cols, "row", axis=0, tiled=True).reshape(-1)
    f32, dma = jnp.float32, pltpu.SemaphoreType.DMA
    vmem, smem = pl.BlockSpec(memory_space=pltpu.VMEM), pl.BlockSpec(memory_space=pltpu.SMEM)
    return pl.pallas_call(
        functools.partial(kernel, n_row, n_col),
        out_shape=jax.ShapeDtypeStruct(x.shape, f32),
        in_specs=[vmem, smem, smem],
        out_specs=vmem,
        scratch_shapes=[
            [pltpu.VMEM((blk, bs, bs), f32)] * groups,
            pltpu.VMEM((n_row // 2, groups, blk // 2, bs, bs), f32),
            pltpu.VMEM((blk, groups, bs, bs), f32),
            pltpu.VMEM((STEPS - 1, blk, groups, bs, bs), f32),
            pltpu.VMEM((STEPS, blk, bs, bs), f32),
            dma((2, groups)), dma((2, groups)), dma((n_row // 2, groups, CHUNKS)), dma((n_row // 2, groups)), dma,
            dma((3, groups)), dma((STEPS - 1, groups)), dma((STEPS,)),
            dma((STEPS, CHUNKS, 2)), dma((STEPS, CHUNKS)),
        ],
        compiler_params=pltpu.CompilerParams(
            collective_id=0, has_side_effects=True, vmem_limit_bytes=56 * 2**20),
    )(x, cols, storage_map.reshape(-1))


def solution(mesh):
    return jax.shard_map(
        functools.partial(shards, mesh.shape["row"], mesh.shape["col"]),
        mesh=mesh,
        in_specs=(P("row", "col", None, None), P("row", "col"), P("row", "col")),
        out_specs=P("row", "col", None, None),
        check_vma=False,
    )
```
